256 devices in a mesh: dp: 8 (over z), tensor: 8 (over y, core), seq: 4 (over x).
Axes of the slice: x: 4, y: 4, z: 8, core: 2. Of those that a mesh axis runs over, the one named last changes fastest.
Arguments:
- hidden: bfloat16 [5120, 16384], P('dp', 'tensor'), may hold values from -6 to 6
- query_weight: bfloat16 [16384, 8, 1024], P('tensor', None, 'seq'), may hold values from -0.046875 to 0.046875
- adapter_down_factor: bfloat16 [128, 64, 16384], P(('dp', 'seq'), None, 'tensor'), may hold values from -0.046875 to 0.046875
- adapter_up_factor: bfloat16 [128, 64, 8, 1024], P(('dp', 'seq'), None, 'tensor'), may hold values from -0.75 to 0.75
- adapter_pool_slot: int32 [128], replicated, may hold values from 0 to 127, as said below
- adapter_per_request: int32 [8, 32], P('dp'), may hold values from 0 to 127, as said below
- incoming_length: int32 [8, 32], P('dp'), may hold values from 1 to 64, 640 in all within a row
- prefix_page_table: int32 [8, 32, 16], P('dp'), may hold values from 0 to 63
- page_used_count: int32 [8, 32], P('dp'), may hold values from 1 to 16
- paged_key_cache: bfloat16 [8, 64, 64, 8, 128], P('dp', 'seq', None, 'tensor'), may hold values from -68 to 68
- paged_value_cache: bfloat16 [8, 64, 64, 8, 128], P('dp', 'seq', None, 'tensor'), may hold values from -6 to 6
- incoming_keys: bfloat16 [5120, 8, 128], P(('dp', 'seq'), 'tensor'), may hold values from -68 to 68
- incoming_values: bfloat16 [5120, 8, 128], P(('dp', 'seq'), 'tensor'), may hold values from -6 to 6
Outputs:
- attention: bfloat16 [5120, 8, 1024], P('dp', 'tensor', 'seq')
The draws below stay inside these ranges and needn't reach their ends.
Inputs may be any that keep to these rules, and one draw needn't show every extreme that they name: Each slot appears once. The pool's slots are held in order by the devices of dp+seq, 4 slots each, so adapter a lies with holder adapter_pool_slot[a] // 4. `adapter_per_request`: among the 32 requests of one group, the named adapters lie with exactly 16 holders, each holding them for exactly 2 of the requests; one adapter may be named by several requests.
All inputs are finite; a program needn't handle non-finite values.
Results may differ from the reference program's by a relative error of at most 0.01.
The reference program's roundings to bfloat16 on the way count: a program that leaves them out, or rounds other values in their place, can miss the bound.
Values may be sent and summed in bfloat16 or wider, within the bound.
A program may use at most 128 MiB of HBM per device.

```python
import math
import jax
import jax.numpy as jnp
import numpy as np
from jax import lax

MODEL_WIDTH = 16384
KEY_HEADS = 8
HEAD_WIDTH = 128
QUERY_GROUP = 8
ADAPTER_RANK = 64
CAP = 2
ADP_DEV = 4
GROUP_REQUESTS = 32
MOSTNEW = 64
TOK_DEV = 640
PAGE = 64
POOL_DEV = 16
MAXP = 16
TOKENS = 5120
OWNERS = 32
ADAPTER_TOTAL = 128
POOL_G = 64
N_DP = 8
N_SEQ = 4


def owner_plan(key):
    slot_lookup = jax.random.permutation(jax.random.fold_in(key, 11), ADAPTER_TOTAL).astype(jnp.int32)
    adapter_at = jnp.argsort(slot_lookup, stable=True).astype(jnp.int32)
    group_keys = jax.random.split(jax.random.fold_in(key, 12), N_DP)

    def one_group(group_key):
        key_owner, key_order, key_local = jax.random.split(group_key, 3)
        owners_order = jax.random.permutation(key_owner, OWNERS).astype(jnp.int32)
        request_order = jax.random.permutation(key_order, GROUP_REQUESTS).astype(jnp.int32)
        owner_of = owners_order[request_order // CAP]
        pick_local = jax.random.randint(key_local, (GROUP_REQUESTS,), 0, ADP_DEV).astype(jnp.int32)
        return adapter_at[owner_of * ADP_DEV + pick_local]
    return (slot_lookup, jax.vmap(one_group)(group_keys).astype(jnp.int32))


def draw_adapter_pool_slot(key, part):
    slot_lookup, requested = owner_plan(key)
    return slot_lookup


def draw_adapter_per_request(key, part):
    slot_lookup, requested = owner_plan(key)
    return requested


def draw_paged_key_cache(key, part):
    key = jax.random.fold_in(key, 3)
    key_entry = jax.random.fold_in(key, 0)
    array_shape = (N_DP, POOL_DEV * N_SEQ, PAGE, KEY_HEADS, HEAD_WIDTH)
    return jnp.clip(jax.random.normal(key_entry, array_shape, jnp.float32), -6.0, 6.0).astype(jnp.bfloat16)


def draw_incoming_keys(key, part):
    key = jax.random.fold_in(key, 4)
    key_entry = jax.random.fold_in(key, 0)
    array_shape = (TOKENS, KEY_HEADS, HEAD_WIDTH)
    return jnp.clip(jax.random.normal(key_entry, array_shape, jnp.float32), -6.0, 6.0).astype(jnp.bfloat16)


def touch_ends(result, key, low, high):
    longest = result.shape.index(max(result.shape))
    spots = []
    for shift in (0, 1):
        where = [jax.random.randint(jax.random.fold_in(key, axis), (), 0, length) for axis, length in enumerate(result.shape)]
        where[longest] = (where[longest] + shift) % result.shape[longest]
        spots.append(tuple(where))
    return result.at[spots[0]].set(low).at[spots[1]].set(high)


def steps_of(own_key, extent, cuts, smallest, high):
    gain = 1.0
    for dim, parts in cuts:
        heights = jax.random.uniform(jax.random.fold_in(jax.random.fold_in(own_key, 6), dim), (parts,), jnp.float32, smallest / len(cuts), high / len(cuts))
        gain = gain * jnp.repeat(jnp.exp(heights), extent[dim] // parts).reshape((-1,) + (1,) * (len(extent) - 1 - dim))
    return gain


def split_up(amount, total, limit, skew):
    weights = [(1 << 20) // math.isqrt(standing ** skew) + 1 for standing in range(2, amount + 1)]
    spare, counts = total - limit - (amount - 1), [1] * (amount - 1)
    while spare > 0:
        candidates = [i for i in range(amount - 1) if counts[i] < limit]
        mass, remaining = sum([weights[i] for i in candidates]), spare
        for i in candidates:
            extra = min(limit - counts[i], max(1, remaining * weights[i] // mass), spare)
            counts[i] = counts[i] + extra
            spare = spare - extra
    return np.array([limit] + counts)


def ragged_sizes(key, count, total, reach, skew):
    if count == 2:
        one = jax.random.randint(key, (), max(1, total - reach), min(reach, total - 1) + 1)
        return jnp.stack([one, total - one])
    sizes = jnp.asarray(split_up(count, total, reach, skew), jnp.int32)
    twos = (count - 1) // 2
    giver, sink = sizes[1:1 + 2 * twos:2], sizes[2:2 + 2 * twos:2]
    room = jnp.minimum(giver - 1, reach - sink)
    moved = jax.random.randint(jax.random.fold_in(key, 1), (twos,), 0, 1 << 20) % (room + 1)
    sizes = sizes.at[1:1 + 2 * twos:2].set(giver - moved).at[2:2 + 2 * twos:2].set(sink + moved)
    return sizes[jax.random.permutation(jax.random.fold_in(key, 2), count)]


def noise(stream_key, shape, width, bound, shards=(), kind=jnp.bfloat16):
    loudness = steps_of(stream_key, shape, shards, -0.22, 0.18) if shards else 1.0
    result = jax.random.normal(stream_key, shape, jnp.float32) * width * loudness
    return jnp.minimum(jnp.maximum(result, -bound), bound).astype(kind)


def setup_inputs(seed: int = 0) -> dict:
    streams_of = jax.random.split(jax.random.key(seed), 14)
    hidden = noise(streams_of[0], (TOKENS, MODEL_WIDTH), 1.0, 6.0, ((0, 8), (1, 8)))
    query_weight = noise(streams_of[1], (MODEL_WIDTH, KEY_HEADS, QUERY_GROUP * HEAD_WIDTH), MODEL_WIDTH ** -0.5, 0.046875, ((0, 8), (2, 4)))
    adapter_down_factor = noise(streams_of[2], (ADAPTER_TOTAL, ADAPTER_RANK, MODEL_WIDTH), MODEL_WIDTH ** -0.5, 0.046875, ((0, 32), (2, 8)))
    adapter_up_factor = noise(streams_of[3], (ADAPTER_TOTAL, ADAPTER_RANK, KEY_HEADS, QUERY_GROUP * HEAD_WIDTH), ADAPTER_RANK ** -0.5, 0.75, ((0, 32), (2, 8)))
    adapter_pool_slot = draw_adapter_pool_slot(jax.random.fold_in(streams_of[13], 71), 0)
    adapter_per_request = draw_adapter_per_request(jax.random.fold_in(streams_of[13], 71), 0)
    incoming_length = jax.vmap(lambda own: ragged_sizes(own, GROUP_REQUESTS, TOK_DEV, MOSTNEW, 2))(jax.random.split(streams_of[6], N_DP)).reshape((N_DP, GROUP_REQUESTS)).astype(jnp.int32)
    prefix_page_table = touch_ends(jax.random.randint(streams_of[7], (N_DP, GROUP_REQUESTS, MAXP), 0, POOL_G), jax.random.fold_in(streams_of[7], 1), 0, POOL_G - 1).astype(jnp.int32)
    page_used_count = touch_ends(jax.random.randint(streams_of[8], (N_DP, GROUP_REQUESTS), 1, MAXP + 1), jax.random.fold_in(streams_of[8], 1), 1, MAXP).astype(jnp.int32)
    paged_key_cache = draw_paged_key_cache(jax.random.fold_in(streams_of[13], 71), 0)
    paged_value_cache = noise(streams_of[10], (N_DP, POOL_G, PAGE, KEY_HEADS, HEAD_WIDTH), 1.0, 6.0, ((0, 8), (1, 4), (3, 8)))
    incoming_keys = draw_incoming_keys(jax.random.fold_in(streams_of[13], 71), 0)
    incoming_values = noise(streams_of[12], (TOKENS, KEY_HEADS, HEAD_WIDTH), 1.0, 6.0, ((0, 32), (1, 8)))
    return {"hidden": hidden, "query_weight": query_weight, "adapter_down_factor": adapter_down_factor, "adapter_up_factor": adapter_up_factor, "adapter_pool_slot": adapter_pool_slot, "adapter_per_request": adapter_per_request, "incoming_length": incoming_length, "prefix_page_table": prefix_page_table, "page_used_count": page_used_count, "paged_key_cache": paged_key_cache, "paged_value_cache": paged_value_cache, "incoming_keys": incoming_keys, "incoming_values": incoming_values}


floor_score = -1e30


def membership(lengths, total_tokens):
    finish = jnp.cumsum(lengths).astype(jnp.int32)
    starts = (finish - lengths).astype(jnp.int32)
    position = jnp.arange(total_tokens, dtype=jnp.int32)
    member = (position[:, None] >= starts[None, :]) & (position[:, None] < finish[None, :])
    return member, starts


def page_membership(member, prefix_page_table, page_used_count, pool_pages):
    active = jnp.arange(prefix_page_table.shape[1], dtype=jnp.int32)[None, :] < page_used_count[:, None]
    listed = jnp.any((prefix_page_table[:, :, None] == jnp.arange(pool_pages, dtype=jnp.int32)[None, None, :]) & active[:, :, None], axis=1)
    return jnp.any(member[:, :, None] & listed[None, :, :], axis=1)


def request_ids(member):
    return jnp.sum(jnp.where(member, jnp.arange(member.shape[1], dtype=jnp.int32)[None, :], 0), axis=1)


def reference(hidden, query_weight, adapter_down_factor, adapter_up_factor, adapter_pool_slot, adapter_per_request, incoming_length, prefix_page_table, page_used_count, paged_key_cache, paged_value_cache, incoming_keys, incoming_values):
    full_width = KEY_HEADS * QUERY_GROUP * HEAD_WIDTH
    w_flat = query_weight.reshape(MODEL_WIDTH, full_width)
    hidden_groups = hidden.reshape(N_DP, TOK_DEV, MODEL_WIDTH)
    keys_groups = incoming_keys.reshape(N_DP, TOK_DEV, KEY_HEADS, HEAD_WIDTH)
    values_groups = incoming_values.reshape(N_DP, TOK_DEV, KEY_HEADS, HEAD_WIDTH)
    score_scale = HEAD_WIDTH ** -0.5

    def one_group(inputs):
        tokens_in, adapters, lengths, listing, counting, pool_keys, pool_values, fresh_keys, fresh_values = inputs
        member, starts = membership(lengths, TOK_DEV)
        slot_lookup = adapter_pool_slot[adapters]
        down_factor_rows = adapter_down_factor[slot_lookup]
        up_factor_rows = adapter_up_factor[slot_lookup].reshape(GROUP_REQUESTS, ADAPTER_RANK, full_width)
        padded = jnp.concatenate([tokens_in, jnp.zeros((MOSTNEW, MODEL_WIDTH), tokens_in.dtype)], axis=0)
        offsets = jnp.arange(MOSTNEW, dtype=jnp.int32)

        def shrink(running, request):
            token_rows = lax.dynamic_slice_in_dim(padded, starts[request], MOSTNEW, 0)
            product = lax.dot_general(token_rows, down_factor_rows[request], (((1,), (1,)), ((), ())), preferred_element_type=jnp.float32)
            product = jnp.where((offsets < lengths[request])[:, None], product, 0.0)
            window = lax.dynamic_slice_in_dim(running, starts[request], MOSTNEW, 0)
            return lax.dynamic_update_slice_in_dim(running, window + product, starts[request], 0), None

        shrunk_all, _ = lax.scan(shrink, jnp.zeros((TOK_DEV + MOSTNEW, ADAPTER_RANK), jnp.float32), jnp.arange(GROUP_REQUESTS, dtype=jnp.int32))
        shrunk = shrunk_all[:TOK_DEV].astype(jnp.bfloat16)
        shrunk_padded = jnp.concatenate([shrunk, jnp.zeros((MOSTNEW, ADAPTER_RANK), jnp.bfloat16)], axis=0)

        def expand(running, request):
            token_rows = lax.dynamic_slice_in_dim(shrunk_padded, starts[request], MOSTNEW, 0)
            product = jnp.dot(token_rows, up_factor_rows[request], preferred_element_type=jnp.float32)
            product = jnp.where((offsets < lengths[request])[:, None], product, 0.0)
            window = lax.dynamic_slice_in_dim(running, starts[request], MOSTNEW, 0)
            return lax.dynamic_update_slice_in_dim(running, window + product, starts[request], 0), None

        adapter_terms, _ = lax.scan(expand, jnp.zeros((TOK_DEV + MOSTNEW, full_width), jnp.float32), jnp.arange(GROUP_REQUESTS, dtype=jnp.int32))
        base_query = jnp.dot(tokens_in, w_flat, preferred_element_type=jnp.float32)
        queries = (base_query + adapter_terms[:TOK_DEV]).astype(jnp.bfloat16)
        queries = lax.optimization_barrier(queries).astype(jnp.float32).reshape(TOK_DEV, KEY_HEADS, QUERY_GROUP, HEAD_WIDTH)

        page_mask = page_membership(member, listing, counting, POOL_DEV * N_SEQ)
        request_of = request_ids(member)
        positions = jnp.arange(TOK_DEV, dtype=jnp.int32)
        causal = (request_of[:, None] == request_of[None, :]) & (positions[None, :] <= positions[:, None])
        allowed = jnp.concatenate([jnp.repeat(page_mask, PAGE, axis=1), causal], axis=1)

        results = []
        for kv_index in range(KEY_HEADS):
            key_rows = jnp.concatenate([pool_keys[:, :, kv_index].reshape(-1, HEAD_WIDTH), fresh_keys[:, kv_index]], axis=0).astype(jnp.float32)
            value_rows = jnp.concatenate([pool_values[:, :, kv_index].reshape(-1, HEAD_WIDTH), fresh_values[:, kv_index]], axis=0).astype(jnp.float32)
            scores = jnp.einsum("thd,kd->thk", queries[:, kv_index], key_rows) * score_scale
            masked = jnp.where(allowed[:, None, :], scores, floor_score)
            row_max = jnp.max(masked, axis=-1, keepdims=True)
            weights = jnp.where(allowed[:, None, :], jnp.exp(masked - row_max), 0.0)
            weight_sum = jnp.sum(weights, axis=-1, keepdims=True)
            rounded = lax.optimization_barrier(weights.astype(jnp.bfloat16)).astype(jnp.float32)
            summed = jnp.einsum("thk,kd->thd", rounded, value_rows)
            results.append((summed / weight_sum).astype(jnp.bfloat16))
        return jnp.stack(results, axis=1).reshape(TOK_DEV, KEY_HEADS, QUERY_GROUP * HEAD_WIDTH)

    outputs = lax.map(one_group, (hidden_groups, adapter_per_request, incoming_length, prefix_page_table, page_used_count, paged_key_cache, paged_value_cache, keys_groups, values_groups))
    return outputs.reshape(TOKENS, KEY_HEADS, QUERY_GROUP * HEAD_WIDTH)
```

```python
import functools
import math

import jax
import jax.numpy as jnp
from jax import lax
from jax.experimental import pallas as pl
from jax.experimental.pallas import tpu as pltpu
from jax.sharding import PartitionSpec as P

MESH = pl.DeviceIdType.MESH
BF16, F32, I32 = jnp.bfloat16, jnp.float32, jnp.int32

TOK = 640
HALF = 320
WIDTH = 2048
QUARTER = 512
COLS = 256
HEAD = 128
RANK = 64
KEYS = 4096
NEW_EACH = 160
WINDOW = 192
CHUNK = 512
TILE = 320
NEGATIVE = -1e30
EXPONENT = HEAD**-0.5 * math.log2(math.e)


def lanes(rows):
    return lax.broadcasted_iota(I32, (rows, 128), 1)


def token_slots(meta, first, rows):
    position = lax.broadcasted_iota(I32, (rows, 128), 0) + first
    inside = (position >= meta[0:1, :]) & (position < meta[1:2, :])
    slot = jnp.where(inside, meta[2:3, :].astype(F32), 0.0)
    return jnp.broadcast_to(jnp.sum(slot, axis=1, keepdims=True), (rows, 128)).astype(I32)


def kernel(
    hidden,
    weight,
    down,
    up,
    meta,
    pages,
    cache_k,
    cache_v,
    new_k,
    new_v,
    out,
    hid,
    chunks,
    wraw,
    wf32,
    wk,
    downs,
    ups,
    metas,
    part_send,
    part_core,
    part_sum,
    part_y,
    query,
    shr,
    shr_core,
    shr_sum,
    shr_y,
    shr_own,
    shr_x,
    shr_all,
    shr_z,
    shr_final,
    shr_packed,
    shr_wide,
    slots_here,
    bias,
    keys,
    values,
    scores,
    load_sem,
    w_sem,
    meta_s,
    meta_r,
    hid_s,
    hid_r,
    up_s,
    up_r,
    x_s,
    x_r,
    core_s,
    core_r,
    y_s,
    y_r,
    red_s,
    red_r,
):
    z = lax.axis_index("dp")
    t = lax.axis_index("tensor")
    x = lax.axis_index("seq")
    y, core = t // 2, t % 2

    def at_z(d):
        return {"dp": lax.rem(z + d + 8, 8)}

    def at_x(d):
        return {"seq": lax.rem(x + d, 4)}

    def at_y(d):
        return {"tensor": lax.rem(y + d, 4) * 2 + core}

    sibling = {"tensor": y * 2 + 1 - core}
    barrier = pltpu.get_barrier_semaphore()
    peers = [at_z(d) for d in range(1, 8)] + [at_x(d) for d in range(1, 4)]
    peers += [at_y(d) for d in range(1, 4)] + [sibling]
    for peer in peers:
        pl.semaphore_signal(barrier, inc=1, device_id=peer, device_id_type=MESH)
    pl.semaphore_wait(barrier, len(peers))

    def send(src, dst, s, r, peer):
        copy = pltpu.make_async_remote_copy(
            src_ref=src, dst_ref=dst, send_sem=s, recv_sem=r, device_id=peer, device_id_type=MESH
        )
        copy.start()
        return copy

    def local(src, dst, sem):
        copy = pltpu.make_async_copy(src, dst, sem)
        copy.start()
        return copy

    pending = []
    quarter = pl.ds(pl.multiple_of(x * QUARTER, QUARTER), QUARTER)

    ring = {}
    for u in range(2):
        rows = pl.ds(u * HALF, HALF)
        for way in range(2):
            ring[way, 1, u] = send(
                hidden.at[rows, quarter],
                chunks.at[z, rows],
                hid_s.at[way, 0, u],
                hid_r.at[way, 0, u],
                at_z(1 - 2 * way),
            )
    meta_copies = [
        send(meta, metas.at[z], meta_s.at[d], meta_r.at[d], at_z(d)) for d in range(1, 8)
    ]
    own = [local(meta, metas.at[z], load_sem.at[0])]
    own_hid = local(hidden, hid, load_sem.at[1])
    own_chunk = local(hidden.at[:, quarter], chunks.at[z], load_sem.at[2])
    w_copies = [
        local(weight.at[pl.ds(i * 256, 256)], wraw.at[pl.ds(i * 256, 256)], w_sem.at[i])
        for i in range(8)
    ]
    mine4 = pl.ds(x * 4, 4)
    down_copies = []
    for d in range(1, 4):
        to = lax.rem(x + d, 4)
        down_copies.append(
            send(
                down.at[:, :, pl.ds(pl.multiple_of(to * QUARTER, QUARTER), QUARTER)],
                downs.at[mine4],
                x_s.at[0, d],
                x_r.at[0, d],
                at_x(d),
            )
        )
    own_down = local(down.at[:, :, quarter], downs.at[mine4], load_sem.at[3])
    up_copies = []
    for h in range(2):
        for d in range(1, 4):
            to = lax.rem(x + d, 4)
            up_copies.append(
                send(
                    up.at[:, :, pl.ds(pl.multiple_of(to * COLS + h * HEAD, HEAD), HEAD)],
                    ups.at[z, h, mine4],
                    x_s.at[1 + h, d],
                    x_r.at[1 + h, d],
                    at_x(d),
                )
            )
        own.append(
            local(
                up.at[:, :, pl.ds(pl.multiple_of(x * COLS + h * HEAD, HEAD), HEAD)],
                ups.at[z, h, mine4],
                load_sem.at[4 + h],
            )
        )

    def serve_hidden(step, u):
        rows = pl.ds(u * HALF, HALF)
        for way in range(2):
            if step == 4 and u != way:
                continue
            ring[way, step, u].wait_recv()
            if step < 3 or (step == 3 and u == way):
                origin = lax.rem(z + (2 * way - 1) * step + 8, 8)
                ring[way, step + 1, u] = send(
                    chunks.at[origin, rows],
                    chunks.at[origin, rows],
                    hid_s.at[way, step, u],
                    hid_r.at[way, step, u],
                    at_z(1 - 2 * way),
                )

    up_ring = {}

    def up_part(origin, h, r):
        return ups.at[origin, h, pl.ds(r * 8, 8)]

    def start_up(h, r):
        for way in range(2):
            up_ring[way, 1, h, r] = send(
                up_part(z, h, r),
                up_part(z, h, r),
                up_s.at[way, 0, h, r],
                up_r.at[way, 0, h, r],
                at_z(1 - 2 * way),
            )

    def serve_up(step, h, r):
        for way in range(2):
            if step == 4 and r != way:
                continue
            up_ring[way, step, h, r].wait_recv()
            if step < 3 or (step == 3 and r == way):
                origin = lax.rem(z + (2 * way - 1) * step + 8, 8)
                up_ring[way, step + 1, h, r] = send(
                    up_part(origin, h, r),
                    up_part(origin, h, r),
                    up_s.at[way, step, h, r],
                    up_r.at[way, step, h, r],
                    at_z(1 - 2 * way),
                )

    for i in range(8):
        w_copies[i].wait()

    @pl.loop(0, 16)
    def _(i):
        first = pl.multiple_of(i * 128, 128)
        wide = wraw[pl.ds(first, 128)].astype(F32).reshape(1024, COLS)
        wf32[pl.ds(0, 1024)] = wide[:, :HEAD]
        wf32[pl.ds(1024, 1024)] = wide[:, HEAD:]
        for k in range(8):
            for g in range(2):
                wk[k, pl.ds(first, 128), pl.ds(g * HEAD, HEAD)] = wf32[
                    pl.ds(g * 1024 + k, 128, stride=8), :
                ].astype(BF16)

    own_hid.wait()

    def product(head, rows):
        return jnp.dot(hid[rows], wk[head], preferred_element_type=F32)

    part_copies = []
    for d in range(4):
        target = lax.rem(y + 1 + d, 4)

        @pl.loop(0, 2)
        def _(i):
            rows = pl.ds(pl.multiple_of(i * HALF, HALF), HALF)
            part_send[d, rows] = product(target * 2 + 1 - core, rows)

        part_copies.append(
            send(part_send.at[d], part_core.at[d], core_s.at[d], core_r.at[d], sibling)
        )
    serve_hidden(1, 0)
    y_copies = []
    for d in range(4):
        target = lax.rem(y + 1 + d, 4)
        part_copies[d].wait_recv()

        @pl.loop(0, 2)
        def _(i):
            rows = pl.ds(pl.multiple_of(i * HALF, HALF), HALF)
            part_sum[d, rows] = product(target * 2 + core, rows) + part_core[d, rows]

        if d < 3:
            y_copies.append(
                send(part_sum.at[d], part_y.at[d], y_s.at[d], y_r.at[d], at_y(1 + d))
            )
    serve_hidden(1, 1)

    for copy in meta_copies:
        copy.wait_recv()
    own[0].wait()
    own_down.wait()
    own_chunk.wait()
    for copy in down_copies:
        copy.wait_recv()

    def shrink(origin):
        origin = lax.rem(origin + 8, 8)
        about = metas[origin]

        def block(first):
            rows = pl.ds(first, 160)
            product = lax.dot_general(
                chunks[origin, rows],
                downs[...].reshape(1024, QUARTER),
                (((1,), (1,)), ((), ())),
                preferred_element_type=F32,
            )
            slot = token_slots(about, first, 160) - z * 16
            half = lanes(160) // RANK
            total = jnp.zeros((160, 128), F32)
            for j in range(8):
                piece = product[:, j * 128 : (j + 1) * 128]
                total = total + jnp.where(slot == 2 * j + half, piece, 0.0)
            return total + pltpu.roll(total, RANK, 1)

        @pl.loop(0, 2)
        def _(i):
            first = pl.multiple_of(i * 160, 160)
            low, high = block(first), block(first + HALF)
            shr[origin, pl.ds(first, 160)] = jnp.where(lanes(160) < RANK, low, high)

    shrink(z)
    shrink(z - 1)
    serve_hidden(2, 0)
    shrink(z + 1)
    own[1].wait()
    own[2].wait()
    for copy in up_copies:
        copy.wait_recv()

    kv_copies = []
    mine_old = pl.ds(pl.multiple_of(x * 1024, 1024), 1024)
    mine_new = pl.ds(pl.multiple_of(KEYS + x * NEW_EACH, 32), NEW_EACH)
    first_lanes = pl.ds(0, HEAD)
    for n, (src, dst) in enumerate(
        (
            (cache_k, keys.at[mine_old, first_lanes]),
            (cache_v, values.at[mine_old]),
            (new_k, keys.at[mine_new, first_lanes]),
            (new_v, values.at[mine_new]),
        )
    ):
        for d in range(1, 4):
            kv_copies.append(send(src, dst, x_s.at[3 + n, d], x_r.at[3 + n, d], at_x(d)))
        own.append(local(src, dst, load_sem.at[6 + n]))
    serve_hidden(2, 1)
    shrink(z - 2)
    shrink(z + 2)

    about = metas[z]
    place = lanes(32)
    listed = jnp.zeros((32, 128), F32)
    for i in range(16):
        listed = jnp.maximum(listed, jnp.where(pages[:, i : i + 1] == place, 1.0, 0.0))
    same = place - 64 == lax.broadcasted_iota(I32, (32, 128), 0)
    listed = jnp.where(same, 1.0, listed)
    listed = jnp.concatenate([listed, jnp.zeros((96, 128), F32)], axis=0).astype(BF16)

    @pl.loop(0, 4)
    def _(i):
        first = pl.multiple_of(i * 160, 160)
        rows = pl.ds(first, 160)
        position = lax.broadcasted_iota(I32, (160, 128), 0) + first
        member = (position >= about[0:1, :]) & (position < about[1:2, :])
        count = jnp.dot(
            jnp.where(member, 1.0, 0.0).astype(BF16), listed, preferred_element_type=F32
        )
        free = (count > 0.5) | (lanes(160) >= 96)
        bias[rows] = jnp.where(free, 0.0, NEGATIVE).astype(BF16)
        slots_here[rows] = token_slots(about, first, 160)
        shifted = (position >= about[3:4, :]) & (position < about[4:5, :])
        keys[pl.ds(pl.multiple_of(KEYS + i * 160, 32), 160), pl.ds(HEAD, 128)] = jnp.where(
            shifted, 1.0, 0.0
        ).astype(BF16)

    @pl.loop(0, 16)
    def _(i):
        first = pl.multiple_of(i * 256, 256)
        page = (lax.broadcasted_iota(I32, (256, 128), 0) + first) // 64
        keys[pl.ds(first, 256), pl.ds(HEAD, 128)] = jnp.where(
            page == lanes(256), 1.0, 0.0
        ).astype(BF16)

    serve_hidden(3, 0)
    start_up(0, 0)
    start_up(0, 1)
    for copy in y_copies:
        copy.wait_recv()

    @pl.loop(0, 2)
    def _(i):
        rows = pl.ds(pl.multiple_of(i * HALF, HALF), HALF)
        total = part_sum[3, rows] + part_y[0, rows] + part_y[1, rows] + part_y[2, rows]
        query[0, rows] = total[:, :HEAD]
        query[1, rows] = total[:, HEAD:]

    serve_hidden(3, 1)
    shrink(z - 3)
    shrink(z + 3)
    serve_hidden(4, 0)
    serve_hidden(4, 1)
    shrink(z + 4)

    other_rows = pl.ds(pl.multiple_of((1 - core) * 160, 32), 160)
    core_rows = pl.ds(pl.multiple_of(core * 160, 32), 160)
    core_copy = send(shr.at[:, other_rows], shr_core, red_s.at[0, 0], red_r.at[0, 0], sibling)
    serve_up(1, 0, 0)
    core_copy.wait_recv()
    shr_sum[...] = shr[:, core_rows] + shr_core[...]
    red_y = []
    for d in range(1, 4):
        rows = pl.ds(pl.multiple_of(lax.rem(y + d, 4) * 40, 8), 40)
        red_y.append(
            send(shr_sum.at[:, rows], shr_y.at[d - 1], red_s.at[1, d], red_r.at[1, d], at_y(d))
        )
    serve_up(1, 0, 1)
    serve_up(2, 0, 0)
    for copy in red_y:
        copy.wait_recv()
    shr_own[...] = (
        shr_sum[:, pl.ds(pl.multiple_of(y * 40, 8), 40)] + shr_y[0] + shr_y[1] + shr_y[2]
    )
    red_x = [
        send(shr_own, shr_x.at[x], red_s.at[2, d], red_r.at[2, d], at_x(d)) for d in range(1, 4)
    ]
    shr_x[x] = shr_own[...]
    start_up(1, 0)
    start_up(1, 1)
    serve_up(2, 0, 1)
    serve_up(3, 0, 0)
    for copy in red_x:
        copy.wait_recv()
    shr_all[...] = (shr_x[0] + shr_x[1] + shr_x[2] + shr_x[3]).astype(BF16).astype(F32)
    red_z = [
        send(
            shr_all.at[lax.rem(z + d, 8)], shr_z.at[d - 1], red_s.at[3, d], red_r.at[3, d], at_z(d)
        )
        for d in range(1, 8)
    ]
    serve_up(3, 0, 1)
    for copy in red_z:
        copy.wait_recv()
    total = shr_all[z]
    for d in range(7):
        total = total + shr_z[d]
    shr_final[...] = total
    final_rows = pl.ds(pl.multiple_of(core * 160 + y * 40, 8), 40)
    red_f = [
        send(
            shr_final, shr_packed.at[final_rows], red_s.at[4, d], red_r.at[4, d], at_y(d)
        )
        for d in range(1, 4)
    ]
    shr_packed[final_rows] = total
    for copy in red_f:
        copy.wait_recv()
    core_final = send(
        shr_packed.at[core_rows], shr_packed.at[core_rows], red_s.at[0, 1], red_r.at[0, 1], sibling
    )
    serve_up(4, 0, 0)
    serve_up(4, 0, 1)
    core_final.wait_recv()
    packed = shr_packed[...]
    turned = pltpu.roll(packed, RANK, 1)
    shr_wide[pl.ds(0, HALF)] = jnp.where(lanes(HALF) < RANK, packed, turned)
    shr_wide[pl.ds(HALF, HALF)] = jnp.where(lanes(HALF) < RANK, turned, packed)

    def expand(origin, h):
        origin = lax.rem(origin + 8, 8)

        @pl.loop(0, 4)
        def _(i):
            rows = pl.ds(pl.multiple_of(i * 160, 160), 160)
            slot = slots_here[rows] - origin * 16
            wide = shr_wide[rows]
            half = lanes(160) // RANK
            spread = jnp.concatenate(
                [jnp.where(slot == 2 * j + half, wide, 0.0).astype(BF16) for j in range(8)], axis=1
            )
            query[h, rows] += jnp.dot(
                spread, ups[origin, h].reshape(1024, HEAD), preferred_element_type=F32
            )

    def attend(h):
        @pl.loop(0, TOK // TILE)
        def _(i):
            first = pl.multiple_of(i * TILE, TILE)
            rows = pl.ds(first, TILE)
            left = jnp.concatenate([query[h, rows].astype(BF16), bias[rows]], axis=1)
            highest = jnp.full((TILE, 128), NEGATIVE, F32)
            for c in range(KEYS // CHUNK):
                piece = lax.dot_general(
                    left,
                    keys[pl.ds(c * CHUNK, CHUNK)],
                    (((1,), (1,)), ((), ())),
                    preferred_element_type=F32,
                )
                scores[:, pl.ds(c * CHUNK, CHUNK)] = piece
                for j in range(CHUNK // 128):
                    highest = jnp.maximum(highest, piece[:, j * 128 : (j + 1) * 128])
            piece = lax.dot_general(
                left,
                keys[pl.ds(KEYS, TOK)],
                (((1,), (1,)), ((), ())),
                preferred_element_type=F32,
            )
            position = lax.broadcasted_iota(I32, (TILE, TOK), 0) + first
            piece = jnp.where(
                lax.broadcasted_iota(I32, (TILE, TOK), 1) <= position, piece, NEGATIVE
            )
            scores[:, pl.ds(KEYS, TOK)] = piece
            for j in range(TOK // 128):
                highest = jnp.maximum(highest, piece[:, j * 128 : (j + 1) * 128])
            top = jnp.broadcast_to(jnp.max(highest, axis=1, keepdims=True), (TILE, 128))
            sums = jnp.zeros((TILE, 128), F32)
            total = jnp.zeros((TILE, HEAD), F32)
            bounds = [(c * CHUNK, CHUNK) for c in range(KEYS // CHUNK)] + [(KEYS, TOK)]
            for begin, size in bounds:
                parts = []
                for j in range(size // 128):
                    e = jnp.exp2((scores[:, pl.ds(begin + j * 128, 128)] - top) * EXPONENT)
                    sums = sums + e
                    parts.append(e.astype(BF16))
                total = total + jnp.dot(
                    jnp.concatenate(parts, axis=1),
                    values[pl.ds(begin, size)],
                    preferred_element_type=F32,
                )
            out[rows, pl.ds(h * HEAD, HEAD)] = (
                total / jnp.sum(sums, axis=1, keepdims=True)
            ).astype(BF16)

    for d in (0, -1, 1):
        expand(z + d, 0)
    serve_up(1, 1, 0)
    serve_up(1, 1, 1)
    for d in (-2, 2, -3, 3, 4):
        expand(z + d, 0)
    serve_up(2, 1, 0)
    serve_up(2, 1, 1)
    for copy in kv_copies:
        copy.wait_recv()
    for copy in own[3:]:
        copy.wait()
    for d in (0, -1, 1, -2, 2):
        expand(z + d, 1)
    serve_up(3, 1, 0)
    serve_up(3, 1, 1)
    for d in (-3, 3):
        expand(z + d, 1)
    attend(0)
    serve_up(4, 1, 0)
    serve_up(4, 1, 1)
    expand(z + 4, 1)
    attend(1)

    for copies in (
        list(ring.values()),
        list(up_ring.values()),
        meta_copies,
        down_copies,
        up_copies,
        part_copies,
        y_copies,
        kv_copies,
        [core_copy],
        red_y,
        red_x,
        red_z,
        red_f,
        [core_final],
    ):
        for copy in copies:
            copy.wait_send()


def body(
    hidden,
    query_weight,
    adapter_down_factor,
    adapter_up_factor,
    adapter_pool_slot,
    adapter_per_request,
    incoming_length,
    prefix_page_table,
    page_used_count,
    paged_key_cache,
    paged_value_cache,
    incoming_keys,
    incoming_values,
):
    lengths = incoming_length[0]
    finish = jnp.cumsum(lengths)
    starts = finish - lengths
    slots = jnp.sum(
        jnp.where(
            adapter_per_request[0][:, None] == jnp.arange(128, dtype=I32)[None, :],
            adapter_pool_slot[None, :],
            0,
        ),
        axis=1,
    )
    low = jnp.pad(jnp.stack([starts, finish, slots]), ((0, 5), (0, 96)))
    high = jnp.pad(jnp.stack([starts, finish]), ((3, 3), (64, 32)))
    meta = low + high
    pages = jnp.where(
        jnp.arange(16, dtype=I32)[None, :] < page_used_count[0][:, None], prefix_page_table[0], -1
    )
    vmem = pl.BlockSpec(memory_space=pltpu.VMEM)
    anywhere = pl.BlockSpec(memory_space=pl.ANY)
    dma = pltpu.SemaphoreType.DMA
    result = pl.pallas_call(
        kernel,
        out_shape=jax.ShapeDtypeStruct((TOK, COLS), BF16),
        in_specs=[anywhere] * 5 + [vmem] + [anywhere] * 4,
        out_specs=vmem,
        scratch_shapes=[
            pltpu.VMEM((TOK, WIDTH), BF16),
            pltpu.VMEM((8, TOK, QUARTER), BF16),
            pltpu.VMEM((WIDTH, 8, COLS), BF16),
            pltpu.VMEM((2048, HEAD), F32),
            pltpu.VMEM((8, WIDTH, COLS), BF16),
            pltpu.VMEM((16, RANK, QUARTER), BF16),
            pltpu.VMEM((8, 2, 16, RANK, HEAD), BF16),
            pltpu.VMEM((8, 8, 128), I32),
            pltpu.VMEM((4, TOK, COLS), F32),
            pltpu.VMEM((4, TOK, COLS), F32),
            pltpu.VMEM((4, TOK, COLS), F32),
            pltpu.VMEM((3, TOK, COLS), F32),
            pltpu.VMEM((2, TOK, HEAD), F32),
            pltpu.VMEM((8, HALF, 128), F32),
            pltpu.VMEM((8, 160, 128), F32),
            pltpu.VMEM((8, 160, 128), F32),
            pltpu.VMEM((3, 8, 40, 128), F32),
            pltpu.VMEM((8, 40, 128), F32),
            pltpu.VMEM((4, 8, 40, 128), F32),
            pltpu.VMEM((8, 40, 128), F32),
            pltpu.VMEM((7, 40, 128), F32),
            pltpu.VMEM((40, 128), F32),
            pltpu.VMEM((HALF, 128), F32),
            pltpu.VMEM((TOK, 128), F32),
            pltpu.VMEM((TOK, 128), I32),
            pltpu.VMEM((TOK, 128), BF16),
            pltpu.VMEM((KEYS + TOK, 2 * HEAD), BF16),
            pltpu.VMEM((KEYS + TOK, HEAD), BF16),
            pltpu.VMEM((TILE, KEYS + TOK), F32),
            dma((10,)),
            dma((8,)),
            dma((8,)),
            dma((8,)),
            dma((2, 4, 2)),
            dma((2, 4, 2)),
            dma((2, 4, 2, 2)),
            dma((2, 4, 2, 2)),
            dma((7, 4)),
            dma((7, 4)),
            dma((4,)),
            dma((4,)),
            dma((3,)),
            dma((3,)),
            dma((5, 8)),
            dma((5, 8)),
        ],
        compiler_params=pltpu.CompilerParams(
            collective_id=0, has_side_effects=True, vmem_limit_bytes=63 << 20
        ),
        name="layer",
    )(
        hidden,
        query_weight,
        adapter_down_factor,
        adapter_up_factor.reshape(4, RANK, 1024),
        meta,
        pages,
        paged_key_cache.reshape(1024, HEAD),
        paged_value_cache.reshape(1024, HEAD),
        incoming_keys.reshape(NEW_EACH, HEAD),
        incoming_values.reshape(NEW_EACH, HEAD),
    )
    return result.reshape(TOK, 1, COLS)


def solution(mesh):
    return jax.shard_map(
        body,
        mesh=mesh,
        in_specs=(
            P("dp", "tensor"),
            P("tensor", None, "seq"),
            P(("dp", "seq"), None, "tensor"),
            P(("dp", "seq"), None, "tensor", None),
            P(),
            P("dp", None),
            P("dp", None),
            P("dp", None, None),
            P("dp", None),
            P("dp", "seq", None, "tensor", None),
            P("dp", "seq", None, "tensor", None),
            P(("dp", "seq"), "tensor", None),
            P(("dp", "seq"), "tensor", None),
        ),
        out_specs=P("dp", "tensor", "seq"),
        check_vma=False,
    )
```

```python
import functools
import math

import jax
import jax.numpy as jnp
from jax import lax
from jax.experimental import pallas as pl
from jax.experimental.pallas import tpu as pltpu
from jax.sharding import PartitionSpec as P

MESH = pl.DeviceIdType.MESH
BF16, F32, I32 = jnp.bfloat16, jnp.float32, jnp.int32

TOK = 640
HALF = 320
WIDTH = 2048
QUARTER = 512
COLS = 256
HEAD = 128
RANK = 64
KEYS = 4096
NEW_EACH = 160
WINDOW = 384
CHUNK = 512
TILE = 320
NEGATIVE = -1e30
ORDER = (0, 1, -1, 2, -2, 3, -3, 4)
EXPONENT = HEAD**-0.5 * math.log2(math.e)


def iota(shape, dimension):
    return lax.broadcasted_iota(I32, shape, dimension)


def as_bf16(condition):
    return jnp.where(condition, 1.0, 0.0).astype(BF16)


def lanes(rows):
    return lax.broadcasted_iota(I32, (rows, 128), 1)


def token_slots(meta, first, rows):
    position = lax.broadcasted_iota(I32, (rows, 128), 0) + first
    inside = (position >= meta[0:1, :]) & (position < meta[1:2, :])
    slot = jnp.where(inside, meta[2:3, :].astype(F32), 0.0)
    return jnp.broadcast_to(jnp.sum(slot, axis=1, keepdims=True), (rows, 128)).astype(I32)


def kernel(
    hidden,
    weight,
    down,
    up,
    pool,
    adapters,
    lengths,
    tables,
    used,
    cache_k,
    cache_v,
    new_k,
    new_v,
    out,
    hid,
    chunks,
    wraw,
    wf32,
    wk,
    downs,
    ups,
    metas,
    part_send,
    part_core,
    part_sum,
    part_y,
    part_relay,
    query,
    shr,
    shr_core,
    shr_sum,
    shr_y,
    shr_x,
    shr_all,
    shr_z,
    shr_packed,
    shr_wide,
    slots_here,
    bias,
    keys,
    values,
    scores,
    load_sem,
    w_sem,
    meta_s,
    meta_r,
    hid_s,
    hid_r,
    up_s,
    up_r,
    x_s,
    x_r,
    core_s,
    core_r,
    y_s,
    y_r,
    red_s,
    red_r,
):
    z = lax.axis_index("dp")
    t = lax.axis_index("tensor")
    x = lax.axis_index("seq")
    y, core = t // 2, t % 2

    def at_z(d):
        return {"dp": lax.rem(z + d + 8, 8)}

    def at_x(d):
        return {"seq": lax.rem(x + d, 4)}

    def at_y(d):
        return {"tensor": lax.rem(y + d, 4) * 2 + core}

    sibling = {"tensor": y * 2 + 1 - core}
    barrier = pltpu.get_barrier_semaphore()
    peers = [at_z(d) for d in range(1, 8)] + [at_x(d) for d in range(1, 4)]
    peers += [at_y(d) for d in range(1, 4)] + [sibling]
    for peer in peers:
        pl.semaphore_signal(barrier, inc=1, device_id=peer, device_id_type=MESH)
    pl.semaphore_wait(barrier, len(peers))

    def send(src, dst, s, r, peer):
        copy = pltpu.make_async_remote_copy(
            src_ref=src, dst_ref=dst, send_sem=s, recv_sem=r, device_id=peer, device_id_type=MESH
        )
        copy.start()
        return copy

    def local(src, dst, sem):
        copy = pltpu.make_async_copy(src, dst, sem)
        copy.start()
        return copy

    quarter = pl.ds(pl.multiple_of(x * QUARTER, QUARTER), QUARTER)

    ring = {}
    for u in range(2):
        rows = pl.ds(u * HALF, HALF)
        for way in range(2):
            ring[way, 1, u] = send(
                hidden.at[rows, quarter],
                chunks.at[z, rows],
                hid_s.at[way, 0, u],
                hid_r.at[way, 0, u],
                at_z(1 - 2 * way),
            )
    row, column = iota((32, 128), 0), iota((32, 128), 1)

    def spread_out(ref, matrix):
        wide = jnp.broadcast_to(ref[...], (8, ref.shape[1])).astype(F32).astype(BF16)
        return jnp.dot(wide, as_bf16(matrix), preferred_element_type=F32)

    finish = spread_out(lengths, (row <= column) & (column < 32))
    starts = spread_out(lengths, (row < column) & (column < 32))
    finish_high = spread_out(lengths, (row <= column - 64) & (column < 96))
    starts_high = spread_out(lengths, (row < column - 64) & (column < 96))
    adapter = spread_out(adapters, row == column)[0:1, :]
    named = iota((128, 128), 0).astype(F32) == adapter
    slots = spread_out(pool, named)
    which = iota((8, 128), 0)
    about = jnp.where(which == 0, starts, 0.0)
    for n, values_here in ((1, finish), (2, slots), (3, starts_high), (4, finish_high)):
        about = jnp.where(which == n, values_here, about)
    metas[z] = about.astype(I32)
    meta_copies = [
        send(metas.at[z], metas.at[z], meta_s.at[d], meta_r.at[d], at_z(d)) for d in range(1, 8)
    ]
    own = []
    own_hid = local(hidden, hid, load_sem.at[1])
    own_chunk = local(hidden.at[:, quarter], chunks.at[z], load_sem.at[2])
    w_copies = [
        local(weight.at[pl.ds(i * 256, 256)], wraw.at[pl.ds(i * 256, 256)], w_sem.at[i])
        for i in range(8)
    ]
    mine4 = pl.ds(x * 4, 4)
    down_copies = []
    for d in range(1, 4):
        to = lax.rem(x + d, 4)
        down_copies.append(
            send(
                down.at[:, :, pl.ds(pl.multiple_of(to * QUARTER, QUARTER), QUARTER)],
                downs.at[mine4],
                x_s.at[0, d],
                x_r.at[0, d],
                at_x(d),
            )
        )
    own_down = local(down.at[:, :, quarter], downs.at[mine4], load_sem.at[3])
    def serve_hidden(step, u):
        rows = pl.ds(u * HALF, HALF)
        for way in range(2):
            if step == 4 and u != way:
                continue
            ring[way, step, u].wait_recv()
            if step < 3 or (step == 3 and u == way):
                origin = lax.rem(z + (2 * way - 1) * step + 8, 8)
                ring[way, step + 1, u] = send(
                    chunks.at[origin, rows],
                    chunks.at[origin, rows],
                    hid_s.at[way, step, u],
                    hid_r.at[way, step, u],
                    at_z(1 - 2 * way),
                )

    up_ring = {}

    def up_part(origin, h, r):
        return ups.at[origin, h, pl.ds(r * 8, 8)]

    def start_up(h, r):
        for way in range(2):
            up_ring[way, 1, h, r] = send(
                up_part(z, h, r),
                up_part(z, h, r),
                up_s.at[way, 0, h, r],
                up_r.at[way, 0, h, r],
                at_z(1 - 2 * way),
            )

    def serve_up(step, h, r):
        for way in range(2):
            if step == 4 and r != way:
                continue
            up_ring[way, step, h, r].wait_recv()
            if step < 3 or (step == 3 and r == way):
                origin = lax.rem(z + (2 * way - 1) * step + 8, 8)
                up_ring[way, step + 1, h, r] = send(
                    up_part(origin, h, r),
                    up_part(origin, h, r),
                    up_s.at[way, step, h, r],
                    up_r.at[way, step, h, r],
                    at_z(1 - 2 * way),
                )

    for i in range(8):
        w_copies[i].wait()

    @pl.loop(0, 16)
    def _(i):
        first = pl.multiple_of(i * 128, 128)
        wide = wraw[pl.ds(first, 128)].astype(F32).reshape(1024, COLS)
        wf32[pl.ds(0, 1024)] = wide[:, :HEAD]
        wf32[pl.ds(1024, 1024)] = wide[:, HEAD:]
        for k in range(8):
            for g in range(2):
                wk[k, pl.ds(first, 128), pl.ds(g * HEAD, HEAD)] = wf32[
                    pl.ds(g * 1024 + k, 128, stride=8), :
                ].astype(BF16)

    own_hid.wait()

    def product(head, rows):
        return jnp.dot(hid[rows], wk[head], preferred_element_type=F32)

    part_copies = []
    for d in (1, 0, 2, 3):
        target = lax.rem(y + 1 + d, 4)

        @pl.loop(0, 2)
        def _(i):
            rows = pl.ds(pl.multiple_of(i * HALF, HALF), HALF)
            part_send[d, rows] = product(target * 2 + 1 - core, rows)

        part_copies.append(
            send(part_send.at[d], part_core.at[d], core_s.at[d], core_r.at[d], sibling)
        )
    serve_hidden(1, 0)
    y_copies = []
    relay_copies = []
    for d in (1, 0, 2, 3):
        target = lax.rem(y + 1 + d, 4)
        part_copies[(1, 0, 2, 3).index(d)].wait_recv()

        @pl.loop(0, 2)
        def _(i):
            rows = pl.ds(pl.multiple_of(i * HALF, HALF), HALF)
            part_sum[d, rows] = product(target * 2 + core, rows) + part_core[d, rows]

        if d == 1:
            for way in range(2):
                rows = pl.ds(way * HALF, HALF)
                relay_copies.append(
                    send(
                        part_sum.at[1, rows],
                        part_relay.at[way],
                        y_s.at[way],
                        y_r.at[way],
                        at_y(1 + 2 * way),
                    )
                )
    for way in range(2):
        rows = pl.ds(way * HALF, HALF)
        relay_copies[way].wait_recv()
        part_sum[2 * way, rows] += part_relay[way]
        y_copies.append(
            send(
                part_sum.at[2 * way],
                part_y.at[way],
                y_s.at[2 + way],
                y_r.at[2 + way],
                at_y(1 + 2 * way),
            )
        )
    serve_hidden(1, 1)

    for copy in meta_copies:
        copy.wait_recv()
    own_down.wait()
    own_chunk.wait()
    for copy in down_copies:
        copy.wait_recv()
    up_copies = []
    for h in range(2):
        for d in range(1, 4):
            to = lax.rem(x + d, 4)
            up_copies.append(
                send(
                    up.at[:, :, pl.ds(pl.multiple_of(to * COLS + h * HEAD, HEAD), HEAD)],
                    ups.at[z, h, mine4],
                    x_s.at[1 + h, d],
                    x_r.at[1 + h, d],
                    at_x(d),
                )
            )
        own.append(
            local(
                up.at[:, :, pl.ds(pl.multiple_of(x * COLS + h * HEAD, HEAD), HEAD)],
                ups.at[z, h, mine4],
                load_sem.at[4 + h],
            )
        )

    def shrink(place):
        origin = lax.rem(z + ORDER[place] + 8, 8)
        about = metas[origin]

        def block(first):
            rows = pl.ds(first, 160)
            product = lax.dot_general(
                chunks[origin, rows],
                downs[...].reshape(1024, QUARTER),
                (((1,), (1,)), ((), ())),
                preferred_element_type=F32,
            )
            slot = token_slots(about, first, 160) - z * 16
            half = lanes(160) // RANK
            total = jnp.zeros((160, 128), F32)
            for j in range(8):
                piece = product[:, j * 128 : (j + 1) * 128]
                total = total + jnp.where(slot == 2 * j + half, piece, 0.0)
            return total + pltpu.roll(total, RANK, 1)

        @pl.loop(0, 2)
        def _(i):
            first = pl.multiple_of(i * 160, 160)
            low, high = block(first), block(first + HALF)
            shr[place, pl.ds(first, 160)] = jnp.where(lanes(160) < RANK, low, high)

    other_rows = pl.ds(pl.multiple_of((1 - core) * 160, 32), 160)
    core_rows = pl.ds(pl.multiple_of(core * 160, 32), 160)
    batches = (pl.ds(0, 5), pl.ds(5, 3))
    red = []

    def finish_all(copies):
        for copy in copies:
            copy.wait_recv()
        red.extend(copies)

    def reduce_core(b):
        return [
            send(
                shr.at[batches[b], other_rows],
                shr_core.at[batches[b]],
                red_s.at[0, b, 0],
                red_r.at[0, b, 0],
                sibling,
            )
        ]

    def reduce_y(b, before):
        finish_all(before)
        batch = batches[b]
        shr_sum[batch] = shr[batch, core_rows] + shr_core[batch]
        copies = []
        for d in range(1, 4):
            rows = pl.ds(pl.multiple_of(lax.rem(y + d, 4) * 40, 8), 40)
            copies.append(
                send(
                    shr_sum.at[batch, rows],
                    shr_y.at[d - 1, batch],
                    red_s.at[1, b, d],
                    red_r.at[1, b, d],
                    at_y(d),
                )
            )
        return copies

    def reduce_x(b, before):
        finish_all(before)
        batch = batches[b]
        mine = shr_sum[batch, pl.ds(pl.multiple_of(y * 40, 8), 40)]
        shr_x[x, batch] = mine + shr_y[0, batch] + shr_y[1, batch] + shr_y[2, batch]
        return [
            send(
                shr_x.at[x, batch],
                shr_x.at[x, batch],
                red_s.at[2, b, d],
                red_r.at[2, b, d],
                at_x(d),
            )
            for d in range(1, 4)
        ]

    def reduce_z(b, before):
        finish_all(before)
        batch = batches[b]
        total = shr_x[0, batch] + shr_x[1, batch] + shr_x[2, batch] + shr_x[3, batch]
        shr_all[batch] = total.astype(BF16).astype(F32)
        return [
            send(
                shr_all.at[place],
                shr_z.at[place],
                red_s.at[3, b, place],
                red_r.at[3, b, place],
                at_z(ORDER[place]),
            )
            for place in ((1, 2, 3, 4) if b == 0 else (5, 6, 7))
        ]

    shrink(0)
    shrink(1)
    serve_hidden(2, 0)
    serve_hidden(2, 1)
    shrink(2)
    own[0].wait()
    own[1].wait()
    for copy in up_copies:
        copy.wait_recv()

    first_lanes = pl.ds(0, HEAD)

    def old_rows(d):
        return pl.ds(pl.multiple_of(lax.rem(x + d, 4) * 1024, 1024), 1024)

    def new_rows(d):
        return pl.ds(pl.multiple_of(KEYS + lax.rem(x + d, 4) * NEW_EACH, 32), NEW_EACH)

    def place_of(n, d):
        rows = old_rows(d) if n < 2 else new_rows(d)
        return keys.at[rows, first_lanes] if n % 2 == 0 else values.at[rows]

    kv_copies = {}
    for n, src in enumerate((cache_k, cache_v, new_k, new_v)):
        for way in range(2):
            kv_copies[n, way] = send(
                src, place_of(n, 0), x_s.at[3 + n, way], x_r.at[3 + n, way], at_x(1 + 2 * way)
            )
        own.append(local(src, place_of(n, 0), load_sem.at[6 + n]))

    def pass_on():
        for n in range(4):
            way = n % 2
            kv_copies[n, way].wait_recv()
            arrived = place_of(n, 3 - 2 * way)
            kv_copies[n, 2] = send(
                arrived, arrived, x_s.at[3 + n, 2], x_r.at[3 + n, 2], at_x(1 + 2 * way)
            )

    shrink(3)
    shrink(4)
    first_core = reduce_core(0)

    about = metas[z]
    row, column = iota((128, 32), 0), iota((128, 32), 1)
    listed = row - 64 == column
    for i in range(16):
        listed = listed | ((tables[i : i + 1, :] == row) & (used[...] > i) & (row < 64))
    listed = as_bf16(listed)

    @pl.loop(0, 4)
    def _(i):
        first = pl.multiple_of(i * 160, 160)
        rows = pl.ds(first, 160)
        position = lax.broadcasted_iota(I32, (160, 128), 0) + first
        member = (position >= about[0:1, :]) & (position < about[1:2, :])
        count = lax.dot_general(
            as_bf16(member)[:, :32], listed, (((1,), (1,)), ((), ())), preferred_element_type=F32
        )
        free = (count > 0.5) | (lanes(160) >= 96)
        bias[rows] = jnp.where(free, 0.0, NEGATIVE).astype(BF16)
        slots_here[rows] = token_slots(about, first, 160)
        shifted = (position >= about[3:4, :]) & (position < about[4:5, :])
        keys[pl.ds(pl.multiple_of(KEYS + i * 160, 32), 160), pl.ds(HEAD, 128)] = jnp.where(
            shifted, 1.0, 0.0
        ).astype(BF16)

    @pl.loop(0, 16)
    def _(i):
        first = pl.multiple_of(i * 256, 256)
        page = (lax.broadcasted_iota(I32, (256, 128), 0) + first) // 64
        keys[pl.ds(first, 256), pl.ds(HEAD, 128)] = jnp.where(
            page == lanes(256), 1.0, 0.0
        ).astype(BF16)

    first_y = reduce_y(0, first_core)
    serve_hidden(3, 0)
    serve_hidden(3, 1)
    start_up(0, 0)
    start_up(0, 1)
    first_x = reduce_x(0, first_y)
    shrink(5)
    shrink(6)
    pass_on()
    start_up(1, 0)
    start_up(1, 1)
    first_z = reduce_z(0, first_x)
    serve_hidden(4, 0)
    serve_hidden(4, 1)
    shrink(7)
    last_core = reduce_core(1)
    serve_up(1, 0, 0)
    serve_up(1, 0, 1)
    last_y = reduce_y(1, last_core)
    serve_up(1, 1, 0)
    serve_up(1, 1, 1)
    last_x = reduce_x(1, last_y)
    serve_up(2, 0, 0)
    serve_up(2, 0, 1)
    last_z = reduce_z(1, last_x)
    finish_all(first_z)
    finish_all(last_z)
    total = shr_all[0]
    for place in range(1, 8):
        total = total + shr_z[place]
    final_rows = pl.ds(pl.multiple_of(core * 160 + y * 40, 8), 40)
    shr_packed[final_rows] = total
    red_f = [
        send(
            shr_packed.at[final_rows],
            shr_packed.at[final_rows],
            red_s.at[4, 0, d],
            red_r.at[4, 0, d],
            at_y(d),
        )
        for d in range(1, 4)
    ]
    serve_up(2, 1, 0)
    serve_up(2, 1, 1)
    finish_all(red_f)
    core_final = send(
        shr_packed.at[core_rows],
        shr_packed.at[core_rows],
        red_s.at[4, 1, 0],
        red_r.at[4, 1, 0],
        sibling,
    )
    serve_up(3, 0, 0)
    serve_up(3, 0, 1)
    for copy in y_copies:
        copy.wait_recv()

    @pl.loop(0, 2)
    def _(i):
        rows = pl.ds(pl.multiple_of(i * HALF, HALF), HALF)
        total = part_sum[3, rows] + part_y[0, rows] + part_y[1, rows]
        query[0, rows] = total[:, :HEAD]
        query[1, rows] = total[:, HEAD:]

    finish_all([core_final])
    packed = shr_packed[...]
    turned = pltpu.roll(packed, RANK, 1)
    shr_wide[pl.ds(0, HALF)] = jnp.where(lanes(HALF) < RANK, packed, turned)
    shr_wide[pl.ds(HALF, HALF)] = jnp.where(lanes(HALF) < RANK, turned, packed)

    def expand(origin, h):
        origin = lax.rem(origin + 8, 8)

        @pl.loop(0, 4)
        def _(i):
            rows = pl.ds(pl.multiple_of(i * 160, 160), 160)
            slot = slots_here[rows] - origin * 16
            wide = shr_wide[rows]
            half = lanes(160) // RANK
            spread = jnp.concatenate(
                [jnp.where(slot == 2 * j + half, wide, 0.0).astype(BF16) for j in range(8)], axis=1
            )
            query[h, rows] += jnp.dot(
                spread, ups[origin, h].reshape(1024, HEAD), preferred_element_type=F32
            )

    def attend(h, i):
        first = i * TILE
        begin_new = max(first - 64, 0)
        rows = pl.ds(first, TILE)
        left = jnp.concatenate([query[h, rows].astype(BF16), bias[rows]], axis=1)
        highest = jnp.full((TILE, 128), NEGATIVE, F32)
        for c in range(KEYS // CHUNK):
            piece = lax.dot_general(
                left,
                keys[pl.ds(c * CHUNK, CHUNK)],
                (((1,), (1,)), ((), ())),
                preferred_element_type=F32,
            )
            scores[:, pl.ds(c * CHUNK, CHUNK)] = piece
            for j in range(CHUNK // 128):
                highest = jnp.maximum(highest, piece[:, j * 128 : (j + 1) * 128])
        piece = lax.dot_general(
            left,
            keys[pl.ds(KEYS + begin_new, WINDOW)],
            (((1,), (1,)), ((), ())),
            preferred_element_type=F32,
        )
        position = lax.broadcasted_iota(I32, (TILE, WINDOW), 0) + first
        piece = jnp.where(
            lax.broadcasted_iota(I32, (TILE, WINDOW), 1) + begin_new <= position, piece, NEGATIVE
        )
        scores[:, pl.ds(KEYS, WINDOW)] = piece
        for j in range(WINDOW // 128):
            highest = jnp.maximum(highest, piece[:, j * 128 : (j + 1) * 128])
        top = jnp.broadcast_to(jnp.max(highest, axis=1, keepdims=True), (TILE, 128))
        sums = jnp.zeros((TILE, 128), F32)
        total = jnp.zeros((TILE, HEAD), F32)
        bounds = [(c * CHUNK, c * CHUNK, CHUNK) for c in range(KEYS // CHUNK)]
        bounds.append((KEYS, KEYS + begin_new, WINDOW))
        for begin, place, size in bounds:
            parts = []
            for j in range(size // 128):
                e = jnp.exp2((scores[:, pl.ds(begin + j * 128, 128)] - top) * EXPONENT)
                sums = sums + e
                parts.append(e.astype(BF16))
            total = total + jnp.dot(
                jnp.concatenate(parts, axis=1),
                values[pl.ds(place, size)],
                preferred_element_type=F32,
            )
        out[rows, pl.ds(h * HEAD, HEAD)] = (
            total / jnp.sum(sums, axis=1, keepdims=True)
        ).astype(BF16)

    for d in (0, -1, 1, -2, 2, -3, 3):
        expand(z + d, 0)
    serve_up(4, 0, 0)
    serve_up(4, 0, 1)
    expand(z + 4, 0)
    for n in range(4):
        kv_copies[n, 1 - n % 2].wait_recv()
        kv_copies[n, 2].wait_recv()
    for copy in own[2:]:
        copy.wait()
    attend(0, 0)
    serve_up(3, 1, 0)
    serve_up(3, 1, 1)
    attend(0, 1)
    for d in (0, -1, 1, -2, 2, -3, 3):
        expand(z + d, 1)
    serve_up(4, 1, 0)
    serve_up(4, 1, 1)
    expand(z + 4, 1)
    attend(1, 0)
    attend(1, 1)

    for copies in (
        list(ring.values()),
        list(up_ring.values()),
        meta_copies,
        down_copies,
        up_copies,
        part_copies,
        y_copies,
        relay_copies,
        list(kv_copies.values()),
        red,
    ):
        for copy in copies:
            copy.wait_send()


def body(
    hidden,
    query_weight,
    adapter_down_factor,
    adapter_up_factor,
    adapter_pool_slot,
    adapter_per_request,
    incoming_length,
    prefix_page_table,
    page_used_count,
    paged_key_cache,
    paged_value_cache,
    incoming_keys,
    incoming_values,
):
    vmem = pl.BlockSpec(memory_space=pltpu.VMEM)
    anywhere = pl.BlockSpec(memory_space=pl.ANY)
    dma = pltpu.SemaphoreType.DMA
    result = pl.pallas_call(
        kernel,
        out_shape=jax.ShapeDtypeStruct((TOK, COLS), BF16),
        in_specs=[anywhere] * 4 + [vmem] * 5 + [anywhere] * 4,
        out_specs=vmem,
        scratch_shapes=[
            pltpu.VMEM((TOK, WIDTH), BF16),
            pltpu.VMEM((8, TOK, QUARTER), BF16),
            pltpu.VMEM((WIDTH, 8, COLS), BF16),
            pltpu.VMEM((2048, HEAD), F32),
            pltpu.VMEM((8, WIDTH, COLS), BF16),
            pltpu.VMEM((16, RANK, QUARTER), BF16),
            pltpu.VMEM((8, 2, 16, RANK, HEAD), BF16),
            pltpu.VMEM((8, 8, 128), I32),
            pltpu.VMEM((4, TOK, COLS), F32),
            pltpu.VMEM((4, TOK, COLS), F32),
            pltpu.VMEM((4, TOK, COLS), F32),
            pltpu.VMEM((2, TOK, COLS), F32),
            pltpu.VMEM((2, HALF, COLS), F32),
            pltpu.VMEM((2, TOK, HEAD), F32),
            pltpu.VMEM((8, HALF, 128), F32),
            pltpu.VMEM((8, 160, 128), F32),
            pltpu.VMEM((8, 160, 128), F32),
            pltpu.VMEM((3, 8, 40, 128), F32),
            pltpu.VMEM((4, 8, 40, 128), F32),
            pltpu.VMEM((8, 40, 128), F32),
            pltpu.VMEM((8, 40, 128), F32),
            pltpu.VMEM((HALF, 128), F32),
            pltpu.VMEM((TOK, 128), F32),
            pltpu.VMEM((TOK, 128), I32),
            pltpu.VMEM((TOK, 128), BF16),
            pltpu.VMEM((KEYS + TOK, 2 * HEAD), BF16),
            pltpu.VMEM((KEYS + TOK, HEAD), BF16),
            pltpu.VMEM((TILE, KEYS + WINDOW), F32),
            dma((10,)),
            dma((8,)),
            dma((8,)),
            dma((8,)),
            dma((2, 4, 2)),
            dma((2, 4, 2)),
            dma((2, 4, 2, 2)),
            dma((2, 4, 2, 2)),
            dma((7, 4)),
            dma((7, 4)),
            dma((4,)),
            dma((4,)),
            dma((4,)),
            dma((4,)),
            dma((5, 2, 8)),
            dma((5, 2, 8)),
        ],
        compiler_params=pltpu.CompilerParams(
            collective_id=0, has_side_effects=True, vmem_limit_bytes=63 << 20
        ),
        name="layer",
    )(
        hidden,
        query_weight,
        adapter_down_factor,
        adapter_up_factor.reshape(4, RANK, 1024),
        adapter_pool_slot.reshape(1, 128),
        adapter_per_request,
        incoming_length,
        prefix_page_table[0].T,
        page_used_count,
        paged_key_cache.reshape(1024, HEAD),
        paged_value_cache.reshape(1024, HEAD),
        incoming_keys.reshape(NEW_EACH, HEAD),
        incoming_values.reshape(NEW_EACH, HEAD),
    )
    return result.reshape(TOK, 1, COLS)


def solution(mesh):
    return jax.shard_map(
        body,
        mesh=mesh,
        in_specs=(
            P("dp", "tensor"),
            P("tensor", None, "seq"),
            P(("dp", "seq"), None, "tensor"),
            P(("dp", "seq"), None, "tensor", None),
            P(),
            P("dp", None),
            P("dp", None),
            P("dp", None, None),
            P("dp", None),
            P("dp", "seq", None, "tensor", None),
            P("dp", "seq", None, "tensor", None),
            P(("dp", "seq"), "tensor", None),
            P(("dp", "seq"), "tensor", None),
        ),
        out_specs=P("dp", "tensor", "seq"),
        check_vma=False,
    )
```

```python
import functools
import math

import jax
import jax.numpy as jnp
from jax import lax
from jax.experimental import pallas as pl
from jax.experimental.pallas import tpu as pltpu
from jax.sharding import PartitionSpec as P

MESH = pl.DeviceIdType.MESH
BF16, F32, I32 = jnp.bfloat16, jnp.float32, jnp.int32

TOK = 640
HALF = 320
WIDTH = 2048
QUARTER = 512
COLS = 256
HEAD = 128
RANK = 64
KEYS = 4096
NEW_EACH = 160
WINDOW = 384
CHUNK = 512
TILE = 320
NEGATIVE = -1e30
ORDER = (0, 1, -1, 2, -2, 3, -3, 4)
EXPONENT = HEAD**-0.5 * math.log2(math.e)


def iota(shape, dimension):
    return lax.broadcasted_iota(I32, shape, dimension)


def as_bf16(condition):
    return jnp.where(condition, 1.0, 0.0).astype(BF16)


def lanes(rows):
    return lax.broadcasted_iota(I32, (rows, 128), 1)


def token_slots(meta, first, rows):
    position = lax.broadcasted_iota(I32, (rows, 128), 0) + first
    inside = (position >= meta[0:1, :]) & (position < meta[1:2, :])
    slot = jnp.where(inside, meta[2:3, :].astype(F32), 0.0)
    return jnp.broadcast_to(jnp.sum(slot, axis=1, keepdims=True), (rows, 128)).astype(I32)


def kernel(
    hidden,
    weight,
    down,
    up,
    pool,
    adapters,
    lengths,
    tables,
    used,
    cache_k,
    cache_v,
    new_k,
    new_v,
    out,
    hid,
    chunks,
    wraw,
    wf32,
    wk,
    downs,
    ups,
    metas,
    part_send,
    part_core,
    part_sum,
    part_y,
    part_relay,
    query,
    shr,
    shr_core,
    shr_sum,
    shr_y,
    shr_x,
    shr_all,
    shr_z,
    shr_packed,
    shr_wide,
    slots_here,
    bias,
    keys,
    values,
    scores,
    load_sem,
    w_sem,
    meta_s,
    meta_r,
    hid_s,
    hid_r,
    up_s,
    up_r,
    x_s,
    x_r,
    core_s,
    core_r,
    y_s,
    y_r,
    red_s,
    red_r,
):
    z = lax.axis_index("dp")
    t = lax.axis_index("tensor")
    x = lax.axis_index("seq")
    y, core = t // 2, t % 2

    def at_z(d):
        return {"dp": lax.rem(z + d + 8, 8)}

    def at_x(d):
        return {"seq": lax.rem(x + d, 4)}

    def at_y(d):
        return {"tensor": lax.rem(y + d, 4) * 2 + core}

    sibling = {"tensor": y * 2 + 1 - core}
    barrier = pltpu.get_barrier_semaphore()
    peers = [at_z(d) for d in range(1, 8)] + [at_x(d) for d in range(1, 4)]
    peers += [at_y(d) for d in range(1, 4)] + [sibling]
    for peer in peers:
        pl.semaphore_signal(barrier, inc=1, device_id=peer, device_id_type=MESH)
    pl.semaphore_wait(barrier, len(peers))

    def send(src, dst, s, r, peer):
        copy = pltpu.make_async_remote_copy(
            src_ref=src, dst_ref=dst, send_sem=s, recv_sem=r, device_id=peer, device_id_type=MESH
        )
        copy.start()
        return copy

    def local(src, dst, sem):
        copy = pltpu.make_async_copy(src, dst, sem)
        copy.start()
        return copy

    quarter = pl.ds(pl.multiple_of(x * QUARTER, QUARTER), QUARTER)

    ring = {}
    for u in range(2):
        rows = pl.ds(u * HALF, HALF)
        for way in range(2):
            ring[way, 1, u] = send(
                hidden.at[rows, quarter],
                chunks.at[z, rows],
                hid_s.at[way, 0, u],
                hid_r.at[way, 0, u],
                at_z(1 - 2 * way),
            )
    row, column = iota((32, 128), 0), iota((32, 128), 1)

    def spread_out(ref, matrix):
        wide = jnp.broadcast_to(ref[...], (8, ref.shape[1])).astype(F32).astype(BF16)
        return jnp.dot(wide, as_bf16(matrix), preferred_element_type=F32)

    finish = spread_out(lengths, (row <= column) & (column < 32))
    starts = spread_out(lengths, (row < column) & (column < 32))
    finish_high = spread_out(lengths, (row <= column - 64) & (column < 96))
    starts_high = spread_out(lengths, (row < column - 64) & (column < 96))
    adapter = spread_out(adapters, row == column)[0:1, :]
    named = iota((128, 128), 0).astype(F32) == adapter
    slots = spread_out(pool, named)
    which = iota((8, 128), 0)
    about = jnp.where(which == 0, starts, 0.0)
    for n, values_here in ((1, finish), (2, slots), (3, starts_high), (4, finish_high)):
        about = jnp.where(which == n, values_here, about)
    metas[z] = about.astype(I32)
    meta_copies = [
        send(metas.at[z], metas.at[z], meta_s.at[d], meta_r.at[d], at_z(d)) for d in range(1, 8)
    ]
    own = []
    own_hid = local(hidden, hid, load_sem.at[1])
    own_chunk = local(hidden.at[:, quarter], chunks.at[z], load_sem.at[2])
    w_copies = [
        local(weight.at[pl.ds(i * 256, 256)], wraw.at[pl.ds(i * 256, 256)], w_sem.at[i])
        for i in range(8)
    ]
    mine4 = pl.ds(x * 4, 4)
    down_copies = []
    for d in range(1, 4):
        to = lax.rem(x + d, 4)
        down_copies.append(
            send(
                down.at[:, :, pl.ds(pl.multiple_of(to * QUARTER, QUARTER), QUARTER)],
                downs.at[mine4],
                x_s.at[0, d],
                x_r.at[0, d],
                at_x(d),
            )
        )
    own_down = local(down.at[:, :, quarter], downs.at[mine4], load_sem.at[3])
    def serve_hidden(step, u):
        rows = pl.ds(u * HALF, HALF)
        for way in range(2):
            if step == 4 and u != way:
                continue
            ring[way, step, u].wait_recv()
            if step < 3 or (step == 3 and u == way):
                origin = lax.rem(z + (2 * way - 1) * step + 8, 8)
                ring[way, step + 1, u] = send(
                    chunks.at[origin, rows],
                    chunks.at[origin, rows],
                    hid_s.at[way, step, u],
                    hid_r.at[way, step, u],
                    at_z(1 - 2 * way),
                )

    up_ring = {}

    def up_part(origin, h, r):
        return ups.at[origin, h, pl.ds(r * 8, 8)]

    def start_up(h, r):
        for way in range(2):
            up_ring[way, 1, h, r] = send(
                up_part(z, h, r),
                up_part(z, h, r),
                up_s.at[way, 0, h, r],
                up_r.at[way, 0, h, r],
                at_z(1 - 2 * way),
            )

    def serve_up(step, h, r):
        for way in range(2):
            if step == 4 and r != way:
                continue
            up_ring[way, step, h, r].wait_recv()
            if step < 3 or (step == 3 and r == way):
                origin = lax.rem(z + (2 * way - 1) * step + 8, 8)
                up_ring[way, step + 1, h, r] = send(
                    up_part(origin, h, r),
                    up_part(origin, h, r),
                    up_s.at[way, step, h, r],
                    up_r.at[way, step, h, r],
                    at_z(1 - 2 * way),
                )

    for i in range(8):
        w_copies[i].wait()

    @pl.loop(0, 16)
    def _(i):
        first = pl.multiple_of(i * 128, 128)
        wide = wraw[pl.ds(first, 128)].astype(F32).reshape(1024, COLS)
        wf32[pl.ds(0, 1024)] = wide[:, :HEAD]
        wf32[pl.ds(1024, 1024)] = wide[:, HEAD:]
        for k in range(8):
            for g in range(2):
                wk[k, pl.ds(first, 128), pl.ds(g * HEAD, HEAD)] = wf32[
                    pl.ds(g * 1024 + k, 128, stride=8), :
                ].astype(BF16)

    own_hid.wait()

    def product(head, rows):
        return jnp.dot(hid[rows], wk[head], preferred_element_type=F32)

    part_copies = []
    for d in (1, 0, 2, 3):
        target = lax.rem(y + 1 + d, 4)

        @pl.loop(0, 2)
        def _(i):
            rows = pl.ds(pl.multiple_of(i * HALF, HALF), HALF)
            part_send[d, rows] = product(target * 2 + 1 - core, rows)

        part_copies.append(
            send(part_send.at[d], part_core.at[d], core_s.at[d], core_r.at[d], sibling)
        )
    serve_hidden(1, 0)
    y_copies = []
    relay_copies = []
    for d in (1, 0, 2, 3):
        target = lax.rem(y + 1 + d, 4)
        part_copies[(1, 0, 2, 3).index(d)].wait_recv()

        @pl.loop(0, 2)
        def _(i):
            rows = pl.ds(pl.multiple_of(i * HALF, HALF), HALF)
            part_sum[d, rows] = product(target * 2 + core, rows) + part_core[d, rows]

        if d == 1:
            for way in range(2):
                rows = pl.ds(way * HALF, HALF)
                relay_copies.append(
                    send(
                        part_sum.at[1, rows],
                        part_relay.at[way],
                        y_s.at[way],
                        y_r.at[way],
                        at_y(1 + 2 * way),
                    )
                )
    for way in range(2):
        rows = pl.ds(way * HALF, HALF)
        relay_copies[way].wait_recv()
        part_sum[2 * way, rows] += part_relay[way]
        y_copies.append(
            send(
                part_sum.at[2 * way],
                part_y.at[way],
                y_s.at[2 + way],
                y_r.at[2 + way],
                at_y(1 + 2 * way),
            )
        )
    serve_hidden(1, 1)

    for copy in meta_copies:
        copy.wait_recv()
    own_down.wait()
    own_chunk.wait()
    for copy in down_copies:
        copy.wait_recv()
    up_copies = []
    for h in range(2):
        for d in range(1, 4):
            to = lax.rem(x + d, 4)
            up_copies.append(
                send(
                    up.at[:, :, pl.ds(pl.multiple_of(to * COLS + h * HEAD, HEAD), HEAD)],
                    ups.at[z, h, mine4],
                    x_s.at[1 + h, d],
                    x_r.at[1 + h, d],
                    at_x(d),
                )
            )
        own.append(
            local(
                up.at[:, :, pl.ds(pl.multiple_of(x * COLS + h * HEAD, HEAD), HEAD)],
                ups.at[z, h, mine4],
                load_sem.at[4 + h],
            )
        )

    def shrink(place):
        origin = lax.rem(z + ORDER[place] + 8, 8)
        about = metas[origin]

        def block(first):
            rows = pl.ds(first, 160)
            product = lax.dot_general(
                chunks[origin, rows],
                downs[...].reshape(1024, QUARTER),
                (((1,), (1,)), ((), ())),
                preferred_element_type=F32,
            )
            slot = token_slots(about, first, 160) - z * 16
            half = lanes(160) // RANK
            total = jnp.zeros((160, 128), F32)
            for j in range(8):
                piece = product[:, j * 128 : (j + 1) * 128]
                total = total + jnp.where(slot == 2 * j + half, piece, 0.0)
            return total + pltpu.roll(total, RANK, 1)

        @pl.loop(0, 2)
        def _(i):
            first = pl.multiple_of(i * 160, 160)
            low, high = block(first), block(first + HALF)
            shr[place, pl.ds(first, 160)] = jnp.where(lanes(160) < RANK, low, high)

    other_rows = pl.ds(pl.multiple_of((1 - core) * 160, 32), 160)
    core_rows = pl.ds(pl.multiple_of(core * 160, 32), 160)
    batches = (pl.ds(0, 5), pl.ds(5, 3))
    red = []

    def finish_all(copies):
        for copy in copies:
            copy.wait_recv()
        red.extend(copies)

    def reduce_core(b):
        return [
            send(
                shr.at[batches[b], other_rows],
                shr_core.at[batches[b]],
                red_s.at[0, b, 0],
                red_r.at[0, b, 0],
                sibling,
            )
        ]

    def reduce_y(b, before):
        finish_all(before)
        batch = batches[b]
        shr_sum[batch] = shr[batch, core_rows] + shr_core[batch]
        copies = []
        for d in range(1, 4):
            rows = pl.ds(pl.multiple_of(lax.rem(y + d, 4) * 40, 8), 40)
            copies.append(
                send(
                    shr_sum.at[batch, rows],
                    shr_y.at[d - 1, batch],
                    red_s.at[1, b, d],
                    red_r.at[1, b, d],
                    at_y(d),
                )
            )
        return copies

    def reduce_x(b, before):
        finish_all(before)
        batch = batches[b]
        mine = shr_sum[batch, pl.ds(pl.multiple_of(y * 40, 8), 40)]
        shr_x[x, batch] = mine + shr_y[0, batch] + shr_y[1, batch] + shr_y[2, batch]
        return [
            send(
                shr_x.at[x, batch],
                shr_x.at[x, batch],
                red_s.at[2, b, d],
                red_r.at[2, b, d],
                at_x(d),
            )
            for d in range(1, 4)
        ]

    def reduce_z(b, before):
        finish_all(before)
        batch = batches[b]
        total = shr_x[0, batch] + shr_x[1, batch] + shr_x[2, batch] + shr_x[3, batch]
        shr_all[batch] = total.astype(BF16).astype(F32)
        return [
            send(
                shr_all.at[place],
                shr_z.at[place],
                red_s.at[3, b, place],
                red_r.at[3, b, place],
                at_z(ORDER[place]),
            )
            for place in ((1, 2, 3, 4) if b == 0 else (5, 6, 7))
        ]

    shrink(0)
    shrink(1)
    serve_hidden(2, 0)
    serve_hidden(2, 1)
    shrink(2)
    own[0].wait()
    own[1].wait()
    for copy in up_copies:
        copy.wait_recv()

    first_lanes = pl.ds(0, HEAD)

    def old_rows(d):
        return pl.ds(pl.multiple_of(lax.rem(x + d, 4) * 1024, 1024), 1024)

    def new_rows(d):
        return pl.ds(pl.multiple_of(KEYS + lax.rem(x + d, 4) * NEW_EACH, 32), NEW_EACH)

    def place_of(n, d):
        rows = old_rows(d) if n < 2 else new_rows(d)
        return keys.at[rows, first_lanes] if n % 2 == 0 else values.at[rows]

    kv_copies = {}
    for n, src in enumerate((cache_k, cache_v, new_k, new_v)):
        for way in range(2):
            kv_copies[n, way] = send(
                src, place_of(n, 0), x_s.at[3 + n, way], x_r.at[3 + n, way], at_x(1 + 2 * way)
            )
        own.append(local(src, place_of(n, 0), load_sem.at[6 + n]))

    def pass_on():
        for n in range(4):
            way = n % 2
            kv_copies[n, way].wait_recv()
            arrived = place_of(n, 3 - 2 * way)
            kv_copies[n, 2] = send(
                arrived, arrived, x_s.at[3 + n, 2], x_r.at[3 + n, 2], at_x(1 + 2 * way)
            )

    shrink(3)
    shrink(4)
    first_core = reduce_core(0)

    about = metas[z]
    row, column = iota((128, 32), 0), iota((128, 32), 1)
    listed = row - 64 == column
    for i in range(16):
        listed = listed | ((tables[i : i + 1, :] == row) & (used[...] > i) & (row < 64))
    listed = as_bf16(listed)

    @pl.loop(0, 4)
    def _(i):
        first = pl.multiple_of(i * 160, 160)
        rows = pl.ds(first, 160)
        position = lax.broadcasted_iota(I32, (160, 128), 0) + first
        member = (position >= about[0:1, :]) & (position < about[1:2, :])
        count = lax.dot_general(
            as_bf16(member)[:, :32], listed, (((1,), (1,)), ((), ())), preferred_element_type=F32
        )
        free = (count > 0.5) | (lanes(160) >= 96)
        bias[rows] = jnp.where(free, 0.0, NEGATIVE).astype(BF16)
        slots_here[rows] = token_slots(about, first, 160)
        shifted = (position >= about[3:4, :]) & (position < about[4:5, :])
        keys[pl.ds(pl.multiple_of(KEYS + i * 160, 32), 160), pl.ds(HEAD, 128)] = jnp.where(
            shifted, 1.0, 0.0
        ).astype(BF16)

    @pl.loop(0, 16)
    def _(i):
        first = pl.multiple_of(i * 256, 256)
        page = (lax.broadcasted_iota(I32, (256, 128), 0) + first) // 64
        keys[pl.ds(first, 256), pl.ds(HEAD, 128)] = jnp.where(
            page == lanes(256), 1.0, 0.0
        ).astype(BF16)

    first_y = reduce_y(0, first_core)
    serve_hidden(3, 0)
    serve_hidden(3, 1)
    start_up(0, 0)
    start_up(0, 1)
    first_x = reduce_x(0, first_y)
    shrink(5)
    shrink(6)
    pass_on()
    for copy in y_copies:
        copy.wait_recv()

    @pl.loop(0, 2)
    def _(i):
        rows = pl.ds(pl.multiple_of(i * HALF, HALF), HALF)
        total = part_sum[3, rows] + part_y[0, rows] + part_y[1, rows]
        query[0, rows] = total[:, :HEAD]
        query[1, rows] = total[:, HEAD:]

    start_up(1, 0)
    start_up(1, 1)
    first_z = reduce_z(0, first_x)
    serve_hidden(4, 0)
    serve_hidden(4, 1)
    shrink(7)
    last_core = reduce_core(1)
    serve_up(1, 0, 0)
    serve_up(1, 0, 1)
    last_y = reduce_y(1, last_core)
    serve_up(1, 1, 0)
    serve_up(1, 1, 1)
    last_x = reduce_x(1, last_y)
    last_z = reduce_z(1, last_x)
    finish_all(first_z)
    finish_all(last_z)
    total = shr_all[0]
    for place in range(1, 8):
        total = total + shr_z[place]
    final_rows = pl.ds(pl.multiple_of(core * 160 + y * 40, 8), 40)
    shr_packed[final_rows] = total
    red_f = [
        send(
            shr_packed.at[final_rows],
            shr_packed.at[final_rows],
            red_s.at[4, 0, d],
            red_r.at[4, 0, d],
            at_y(d),
        )
        for d in range(1, 4)
    ]
    finish_all(red_f)
    core_final = send(
        shr_packed.at[core_rows],
        shr_packed.at[core_rows],
        red_s.at[4, 1, 0],
        red_r.at[4, 1, 0],
        sibling,
    )
    serve_up(2, 0, 0)
    finish_all([core_final])
    serve_up(2, 0, 1)
    packed = shr_packed[...]
    turned = pltpu.roll(packed, RANK, 1)
    shr_wide[pl.ds(0, HALF)] = jnp.where(lanes(HALF) < RANK, packed, turned)
    shr_wide[pl.ds(HALF, HALF)] = jnp.where(lanes(HALF) < RANK, turned, packed)

    def expand(origin, h):
        origin = lax.rem(origin + 8, 8)

        @pl.loop(0, 4)
        def _(i):
            rows = pl.ds(pl.multiple_of(i * 160, 160), 160)
            slot = slots_here[rows] - origin * 16
            wide = shr_wide[rows]
            half = lanes(160) // RANK
            spread = jnp.concatenate(
                [jnp.where(slot == 2 * j + half, wide, 0.0).astype(BF16) for j in range(8)], axis=1
            )
            query[h, rows] += jnp.dot(
                spread, ups[origin, h].reshape(1024, HEAD), preferred_element_type=F32
            )

    def attend(h, i):
        first = i * TILE
        begin_new = max(first - 64, 0)
        rows = pl.ds(first, TILE)
        left = jnp.concatenate([query[h, rows].astype(BF16), bias[rows]], axis=1)
        highest = jnp.full((TILE, 128), NEGATIVE, F32)
        for c in range(KEYS // CHUNK):
            piece = lax.dot_general(
                left,
                keys[pl.ds(c * CHUNK, CHUNK)],
                (((1,), (1,)), ((), ())),
                preferred_element_type=F32,
            )
            scores[:, pl.ds(c * CHUNK, CHUNK)] = piece
            for j in range(CHUNK // 128):
                highest = jnp.maximum(highest, piece[:, j * 128 : (j + 1) * 128])
        piece = lax.dot_general(
            left,
            keys[pl.ds(KEYS + begin_new, WINDOW)],
            (((1,), (1,)), ((), ())),
            preferred_element_type=F32,
        )
        position = lax.broadcasted_iota(I32, (TILE, WINDOW), 0) + first
        piece = jnp.where(
            lax.broadcasted_iota(I32, (TILE, WINDOW), 1) + begin_new <= position, piece, NEGATIVE
        )
        scores[:, pl.ds(KEYS, WINDOW)] = piece
        for j in range(WINDOW // 128):
            highest = jnp.maximum(highest, piece[:, j * 128 : (j + 1) * 128])
        top = jnp.broadcast_to(jnp.max(highest, axis=1, keepdims=True), (TILE, 128))
        sums = jnp.zeros((TILE, 128), F32)
        total = jnp.zeros((TILE, HEAD), F32)
        bounds = [(c * CHUNK, c * CHUNK, CHUNK) for c in range(KEYS // CHUNK)]
        bounds.append((KEYS, KEYS + begin_new, WINDOW))
        for begin, place, size in bounds:
            parts = []
            for j in range(size // 128):
                e = jnp.exp2((scores[:, pl.ds(begin + j * 128, 128)] - top) * EXPONENT)
                sums = sums + e
                parts.append(e.astype(BF16))
            total = total + jnp.dot(
                jnp.concatenate(parts, axis=1),
                values[pl.ds(place, size)],
                preferred_element_type=F32,
            )
        out[rows, pl.ds(h * HEAD, HEAD)] = (
            total / jnp.sum(sums, axis=1, keepdims=True)
        ).astype(BF16)

    serve_up(2, 1, 0)
    serve_up(2, 1, 1)
    for n in range(4):
        kv_copies[n, 1 - n % 2].wait_recv()
        kv_copies[n, 2].wait_recv()
    for copy in own[2:]:
        copy.wait()
    for d in (0, -1, 1, -2, 2):
        expand(z + d, 0)
    serve_up(3, 0, 0)
    serve_up(3, 0, 1)
    for d in (0, -1, 1, -2, 2):
        expand(z + d, 1)
    serve_up(3, 1, 0)
    serve_up(3, 1, 1)
    for d in (-3, 3):
        expand(z + d, 0)
        expand(z + d, 1)
    serve_up(4, 0, 0)
    serve_up(4, 0, 1)
    expand(z + 4, 0)
    attend(0, 0)
    attend(0, 1)
    serve_up(4, 1, 0)
    serve_up(4, 1, 1)
    expand(z + 4, 1)
    attend(1, 0)
    attend(1, 1)

    for copies in (
        list(ring.values()),
        list(up_ring.values()),
        meta_copies,
        down_copies,
        up_copies,
        part_copies,
        y_copies,
        relay_copies,
        list(kv_copies.values()),
        red,
    ):
        for copy in copies:
            copy.wait_send()


def body(
    hidden,
    query_weight,
    adapter_down_factor,
    adapter_up_factor,
    adapter_pool_slot,
    adapter_per_request,
    incoming_length,
    prefix_page_table,
    page_used_count,
    paged_key_cache,
    paged_value_cache,
    incoming_keys,
    incoming_values,
):
    vmem = pl.BlockSpec(memory_space=pltpu.VMEM)
    anywhere = pl.BlockSpec(memory_space=pl.ANY)
    dma = pltpu.SemaphoreType.DMA
    result = pl.pallas_call(
        kernel,
        out_shape=jax.ShapeDtypeStruct((TOK, COLS), BF16),
        in_specs=[anywhere] * 4 + [vmem] * 5 + [anywhere] * 4,
        out_specs=vmem,
        scratch_shapes=[
            pltpu.VMEM((TOK, WIDTH), BF16),
            pltpu.VMEM((8, TOK, QUARTER), BF16),
            pltpu.VMEM((WIDTH, 8, COLS), BF16),
            pltpu.VMEM((2048, HEAD), F32),
            pltpu.VMEM((8, WIDTH, COLS), BF16),
            pltpu.VMEM((16, RANK, QUARTER), BF16),
            pltpu.VMEM((8, 2, 16, RANK, HEAD), BF16),
            pltpu.VMEM((8, 8, 128), I32),
            pltpu.VMEM((4, TOK, COLS), F32),
            pltpu.VMEM((4, TOK, COLS), F32),
            pltpu.VMEM((4, TOK, COLS), F32),
            pltpu.VMEM((2, TOK, COLS), F32),
            pltpu.VMEM((2, HALF, COLS), F32),
            pltpu.VMEM((2, TOK, HEAD), F32),
            pltpu.VMEM((8, HALF, 128), F32),
            pltpu.VMEM((8, 160, 128), F32),
            pltpu.VMEM((8, 160, 128), F32),
            pltpu.VMEM((3, 8, 40, 128), F32),
            pltpu.VMEM((4, 8, 40, 128), F32),
            pltpu.VMEM((8, 40, 128), F32),
            pltpu.VMEM((8, 40, 128), F32),
            pltpu.VMEM((HALF, 128), F32),
            pltpu.VMEM((TOK, 128), F32),
            pltpu.VMEM((TOK, 128), I32),
            pltpu.VMEM((TOK, 128), BF16),
            pltpu.VMEM((KEYS + TOK, 2 * HEAD), BF16),
            pltpu.VMEM((KEYS + TOK, HEAD), BF16),
            pltpu.VMEM((TILE, KEYS + WINDOW), F32),
            dma((10,)),
            dma((8,)),
            dma((8,)),
            dma((8,)),
            dma((2, 4, 2)),
            dma((2, 4, 2)),
            dma((2, 4, 2, 2)),
            dma((2, 4, 2, 2)),
            dma((7, 4)),
            dma((7, 4)),
            dma((4,)),
            dma((4,)),
            dma((4,)),
            dma((4,)),
            dma((5, 2, 8)),
            dma((5, 2, 8)),
        ],
        compiler_params=pltpu.CompilerParams(
            collective_id=0, has_side_effects=True, vmem_limit_bytes=63 << 20
        ),
        name="layer",
    )(
        hidden,
        query_weight,
        adapter_down_factor,
        adapter_up_factor.reshape(4, RANK, 1024),
        adapter_pool_slot.reshape(1, 128),
        adapter_per_request,
        incoming_length,
        prefix_page_table[0].T,
        page_used_count,
        paged_key_cache.reshape(1024, HEAD),
        paged_value_cache.reshape(1024, HEAD),
        incoming_keys.reshape(NEW_EACH, HEAD),
        incoming_values.reshape(NEW_EACH, HEAD),
    )
    return result.reshape(TOK, 1, COLS)


def solution(mesh):
    return jax.shard_map(
        body,
        mesh=mesh,
        in_specs=(
            P("dp", "tensor"),
            P("tensor", None, "seq"),
            P(("dp", "seq"), None, "tensor"),
            P(("dp", "seq"), None, "tensor", None),
            P(),
            P("dp", None),
            P("dp", None),
            P("dp", None, None),
            P("dp", None),
            P("dp", "seq", None, "tensor", None),
            P("dp", "seq", None, "tensor", None),
            P(("dp", "seq"), "tensor", None),
            P(("dp", "seq"), "tensor", None),
        ),
        out_specs=P("dp", "tensor", "seq"),
        check_vma=False,
    )
```
